128 devices in a mesh: clip: 4 (over z), frame: 8 (over x, core), row: 4 (over y).
Axes of the slice: x: 4, y: 4, z: 4, core: 2. Of those that a mesh axis runs over, the one named last changes fastest.
Arguments:
- latents: bfloat16 [256, 16, 40, 512], P(('clip', 'frame'), 'row'), parts along dimension 0, may hold values from -12 to 12
- hidden: bfloat16 [256, 16, 40, 512], P(('clip', 'frame'), 'row'), parts along dimension 0, may hold values from -12 to 12
- norm_gain: float32 [512], replicated, may hold values from 0.1 to 1.9
- norm_bias: float32 [512], replicated, may hold values from -3 to 3
- conv_weight: bfloat16 [3, 3, 3, 512, 512], replicated, may hold values from -0.0546875 to 0.0546875
Outputs:
- block_out: bfloat16 [256, 16, 40, 512], P(('clip', 'frame'), 'row'), parts along dimension 0
The draws below stay inside these ranges and needn't reach their ends.
There are 4 independent parts, one for each index of `clip`. The reference program is written for one: setup_inputs(seed, part) draws one part's arguments, and reference() takes and returns one part's arrays. A program takes and returns all parts, laid end to end along the dimension named above; an argument that names none is the same for every part. Nothing has to cross between parts.
All inputs are finite; a program needn't handle non-finite values.
Results may differ from the reference program's by a relative error of at most 0.0013.
The reference program's roundings to bfloat16 on the way (of `act`) count: a program that leaves them out, or rounds other values in their place, can miss the bound.
Values may be sent and summed in bfloat16 or wider, within the bound.
No kernel may reach another device: no remote copies, remote signals or barrier semaphores. Data moves between devices by JAX's collectives and lax.ppermute only.
A program may use at most 192 MiB of HBM per device.

```python
import jax
import jax.numpy as jnp
from jax import lax

C = 512
GROUPS = 32
COLS = 40
FRAMES = 64
ROWS = 16


def normal_field(key):
    key_base, key_rough, key_chan = jax.random.split(key, 3)
    shape = (FRAMES, ROWS, COLS, C)
    frame_pos = (jnp.arange(FRAMES, dtype=jnp.float32) / max(FRAMES - 1, 1)).reshape(-1, 1, 1, 1)
    row_pos = (jnp.arange(ROWS, dtype=jnp.float32) / max(ROWS - 1, 1)).reshape(1, -1, 1, 1)
    scale = 0.4 * jnp.power(3.0, frame_pos) * jnp.power(3.0, row_pos)
    rough = jax.random.uniform(key_rough, (FRAMES, ROWS, COLS, 1), jnp.float32, 0.5, 1.5)
    channel = jnp.exp(jax.random.uniform(key_chan, (C,), jnp.float32, -0.7, 0.7))
    base = jax.random.normal(key_base, shape, jnp.float32)
    return jnp.clip(base * scale * rough * channel, -12.0, 12.0)


def draw_latents(key, part):
    key = jax.random.fold_in(key, 11)
    return normal_field(key).astype(jnp.bfloat16)


def draw_hidden(key, part):
    key = jax.random.fold_in(key, 23)
    return normal_field(key).astype(jnp.bfloat16)


def scatter_about(own_key, extent, width, most, kind=jnp.bfloat16):
    values = jax.random.normal(own_key, extent, jnp.float32) * width
    return jnp.minimum(jnp.maximum(values, -most), most).astype(kind)


def setup_inputs(seed: int = 0, part: int = 0) -> dict:
    key_of = jax.random.split(jax.random.key(seed), 6)
    own_keys = jax.random.split(jax.random.fold_in(key_of[5], part), 6)
    latents = draw_latents(jax.random.fold_in(jax.random.fold_in(key_of[5], part), 71), part)
    hidden = draw_hidden(jax.random.fold_in(jax.random.fold_in(key_of[5], part), 71), part)
    norm_gain = jnp.clip(1.0 + 0.18 * jax.random.normal(key_of[2], (C,), jnp.float32), 0.1, 1.9)
    norm_bias = scatter_about(key_of[3], (C,), 0.5, 3.0, jnp.float32)
    conv_weight = scatter_about(key_of[4], (3, 3, 3, C, C), (27 * C) ** -0.5, 0.0546875)
    return {"latents": latents, "hidden": hidden, "norm_gain": norm_gain, "norm_bias": norm_bias, "conv_weight": conv_weight}


def group_norm(values, gain, bias):
    flat = values.astype(jnp.float32).reshape(-1, GROUPS, C // GROUPS)
    mean = lax.optimization_barrier(jnp.mean(flat, axis=(0, 2), keepdims=True))
    spread = lax.optimization_barrier(jnp.mean((flat - mean) ** 2, axis=(0, 2), keepdims=True))
    normed = (flat - mean) / jnp.sqrt(spread + 1e-06)
    return normed.reshape(values.shape) * gain + bias

def convolve(act, weight):
    nframes, nrows, ncols = (act.shape[0], act.shape[1], act.shape[2])
    lead = jnp.concatenate([act[:1], act[:1], act], axis=0)
    padded = jnp.pad(lead, ((0, 0), (1, 1), (1, 1), (0, 0)))
    total = jnp.zeros((nframes * nrows * ncols, C), jnp.float32)
    for p in range(3):
        for q in range(3):
            for r in range(3):
                slab = padded[p:p + nframes, q:q + nrows, r:r + ncols].reshape(-1, C)
                total = total + jnp.dot(slab, weight[p, q, r], preferred_element_type=jnp.float32)
    return total.reshape(nframes, nrows, ncols, C)

def reference(latents, hidden, norm_gain, norm_bias, conv_weight):
    act = jax.nn.silu(group_norm(hidden, norm_gain, norm_bias)).astype(jnp.bfloat16)
    result = latents.astype(jnp.float32) + convolve(act, conv_weight)
    return result.astype(jnp.bfloat16)
```

```python
import functools

import jax
import jax.numpy as jnp
from jax import lax
from jax.experimental import pallas as pl
from jax.experimental.pallas import tpu as pltpu
from jax.sharding import PartitionSpec as P

C = 512
MEMBERS = 16
FRAMES = 8
ROWS = 4
COLS = 40
OWN = ROWS * COLS
TALL = (ROWS + 2) * COLS
BLOCK = 2
VMEM = pl.BlockSpec(memory_space=pltpu.VMEM)


def stats_kernel(own, out):
    values = own[...].reshape(FRAMES * OWN, C).astype(jnp.float32)
    mean = jnp.sum(values, axis=0, keepdims=True) * (1.0 / (FRAMES * OWN))
    centered = own[...].reshape(FRAMES * OWN, C).astype(jnp.float32) - mean
    spread = jnp.sum(centered * centered, axis=0, keepdims=True)
    out[...] = jnp.concatenate([mean, spread], axis=0)


def local_stats(own):
    return pl.pallas_call(
        stats_kernel,
        out_shape=jax.ShapeDtypeStruct((2, C), jnp.float32),
        in_specs=[VMEM],
        out_specs=VMEM,
        compiler_params=pltpu.CompilerParams(vmem_limit_bytes=16 * 2**20),
    )(own)


def merge_stats(pairs):
    devices = pairs.shape[0]
    cells = FRAMES * OWN
    means = pairs[:, 0]
    mean = jnp.sum(means, axis=0, keepdims=True) * (1.0 / devices)
    off = means - mean
    spread = jnp.sum(pairs[:, 1] + off * off * float(cells), axis=0, keepdims=True)
    both = jnp.concatenate([mean, spread], axis=0)
    lane = lax.broadcasted_iota(jnp.int32, (2, C), 1)
    count = float(cells * devices)
    step = 1
    while step < MEMBERS:
        other = jnp.where((lane & step) != 0, pltpu.roll(both, step, 1), pltpu.roll(both, C - step, 1))
        gap = both[0:1] - other[0:1]
        mean = 0.5 * (both[0:1] + other[0:1])
        spread = both[1:2] + other[1:2] + gap * gap * (0.5 * count)
        both = jnp.concatenate([mean, spread], axis=0)
        count *= 2.0
        step *= 2
    return both[0:1], both[1:2] * (1.0 / count)


def conv_kernel(place, pairs, gain, bias, own, prev, up, down, up_prev, down_prev, latents, weight, out, tall, flat, held, sums, sems):
    def fetch(p, q):
        return pltpu.make_async_copy(weight.at[p, q], held.at[3 * p + q], sems.at[3 * p + q])

    for p in range(3):
        for q in range(3):
            fetch(p, q).start()

    mean, variance = merge_stats(pairs[...])
    scale = gain[...] / jnp.sqrt(variance + 1e-06)
    shift = bias[...]
    first = place[0] == 0
    keep_up = jnp.where(place[1] == 0, 0.0, 1.0)
    keep_down = jnp.where(place[1] == 3, 0.0, 1.0)

    def activate(values):
        normed = (values.astype(jnp.float32) - mean) * scale + shift
        half = 0.5 * normed
        return half + half * jnp.tanh(half)

    def frame(s):
        if s < 2:
            middle = jnp.where(first, own[0], prev[s])
            above = jnp.where(first, up[0], up_prev[s])
            below = jnp.where(first, down[0], down_prev[s])
        else:
            middle, above, below = own[s - 2], up[s - 2], down[s - 2]
        middle = activate(middle)
        above = activate(above) * keep_up
        below = activate(below) * keep_down
        flat[s] = middle.astype(jnp.bfloat16)
        tall[s] = jnp.concatenate([above, middle, below], axis=0).astype(jnp.bfloat16)

    def slab(s, q):
        if q == 1:
            part = flat[s : s + BLOCK]
        else:
            part = tall[s : s + BLOCK, q * COLS : q * COLS + OWN]
        return part.reshape(BLOCK * OWN, C)

    cells = BLOCK * OWN
    column = lax.rem(lax.broadcasted_iota(jnp.int32, (cells, 1), 0), COLS)
    for s in range(BLOCK + 2):
        frame(s)
    for t in range(0, FRAMES, BLOCK):
        for p in range(3):
            for q in range(3):
                if t == 0:
                    fetch(p, q).wait()
                part = slab(t + p, q)
                for r in range(3):
                    term = jnp.dot(part, held[3 * p + q, r], preferred_element_type=jnp.float32)
                    if p == 0 and q == 0:
                        sums[r] = term
                    else:
                        sums[r] += term
        left = jnp.where(column == 0, 0.0, pltpu.roll(sums[0], 1, 0))
        right = jnp.where(column == COLS - 1, 0.0, pltpu.roll(sums[2], cells - 1, 0))
        total = left + sums[1] + right + latents[t : t + BLOCK].reshape(cells, C).astype(jnp.float32)
        out[t : t + BLOCK] = total.astype(jnp.bfloat16).reshape(BLOCK, OWN, C)
        for s in range(t + BLOCK + 2, min(t + 2 * BLOCK + 2, FRAMES + 2)):
            frame(s)


def convolve(place, pairs, gain, bias, own, halos, latents, weight):
    return pl.pallas_call(
        conv_kernel,
        out_shape=jax.ShapeDtypeStruct((FRAMES, OWN, C), jnp.bfloat16),
        in_specs=[pl.BlockSpec(memory_space=pltpu.SMEM)] + [VMEM] * 10 + [pl.BlockSpec(memory_space=pl.ANY)],
        out_specs=VMEM,
        scratch_shapes=[
            pltpu.VMEM((FRAMES + 2, TALL, C), jnp.bfloat16),
            pltpu.VMEM((FRAMES + 2, OWN, C), jnp.bfloat16),
            pltpu.VMEM((9, 3, C, C), jnp.bfloat16),
            pltpu.VMEM((3, BLOCK * OWN, C), jnp.float32),
            pltpu.SemaphoreType.DMA((9,)),
        ],
        compiler_params=pltpu.CompilerParams(vmem_limit_bytes=56 * 2**20),
    )(place, pairs, gain, bias, own, *halos, latents, weight)


def send(block, by_frame, by_row):
    frames, rows = lax.axis_size("frame"), lax.axis_size("row")
    pairs = []
    for f in range(frames):
        for r in range(rows):
            g, s = f + by_frame, r + by_row
            if 0 <= g < frames and 0 <= s < rows:
                pairs.append((f * rows + r, g * rows + s))
    return lax.ppermute(block, ("frame", "row"), pairs)


def shards(latents, hidden, norm_gain, norm_bias, conv_weight):
    own = hidden.reshape(FRAMES, OWN, C)
    last_row, first_row = own[:, OWN - COLS :], own[:, :COLS]
    up = send(last_row, 0, 1)
    down = send(first_row, 0, -1)
    prev = send(own[-2:], 1, 0)
    up_prev = send(last_row[-2:], 1, 1)
    down_prev = send(first_row[-2:], 1, -1)
    stats = local_stats(own)
    members = lax.axis_size("frame") * lax.axis_size("row")
    copies = jnp.broadcast_to(stats[None], (members, 2, C))
    pairs = lax.all_to_all(copies, ("frame", "row"), 0, 0, tiled=True)
    place = jnp.stack([lax.axis_index("frame"), lax.axis_index("row")]).astype(jnp.int32)
    result = convolve(
        place,
        pairs,
        norm_gain.reshape(1, C),
        norm_bias.reshape(1, C),
        own,
        (prev, up, down, up_prev, down_prev),
        latents.reshape(FRAMES, OWN, C),
        conv_weight,
    )
    return result.reshape(FRAMES, ROWS, COLS, C)


def solution(mesh):
    in_specs = (
        P(("clip", "frame"), "row", None, None),
        P(("clip", "frame"), "row", None, None),
        P(),
        P(),
        P(),
    )
    out_specs = P(("clip", "frame"), "row", None, None)
    return jax.shard_map(shards, mesh=mesh, in_specs=in_specs, out_specs=out_specs, check_vma=False)
```

```python
import functools

import jax
import jax.numpy as jnp
from jax import lax
from jax.experimental import pallas as pl
from jax.experimental.pallas import tpu as pltpu
from jax.sharding import PartitionSpec as P

C = 512
MEMBERS = 16
FRAMES = 8
ROWS = 4
COLS = 40
OWN = ROWS * COLS
INNER = 2 * COLS
BLOCK = 4
ROW_SHARDS = 4
WINDOW = 3
TAPS = 9
VMEM = pl.BlockSpec(memory_space=pltpu.VMEM)


HBM = pl.BlockSpec(memory_space=pltpu.HBM)
SMALL = pl.BlockSpec(memory_space=pltpu.SMEM)
WINDOWED = FRAMES + 2


def bf16(*shape):
    return jax.ShapeDtypeStruct(shape, jnp.bfloat16)


def stats_kernel(own, out, tail):
    values = own[...].reshape(FRAMES * OWN, C).astype(jnp.float32)
    mean = jnp.sum(values, axis=0, keepdims=True) * (1.0 / (FRAMES * OWN))
    centered = own[...].reshape(FRAMES * OWN, C).astype(jnp.float32) - mean
    spread = jnp.sum(centered * centered, axis=0, keepdims=True)
    both = jnp.concatenate([mean, spread], axis=0)
    out[...] = jnp.broadcast_to(both[None], out.shape)
    tail[...] = own[FRAMES - 2 :]


def local_stats(own, copies):
    return pl.pallas_call(
        stats_kernel,
        out_shape=(jax.ShapeDtypeStruct((copies, 2, C), jnp.float32), bf16(2, OWN, C)),
        in_specs=[VMEM],
        out_specs=(VMEM, VMEM),
        compiler_params=pltpu.CompilerParams(vmem_limit_bytes=8 * 2**20),
        cost_estimate=pl.CostEstimate(flops=4 * 10**9, bytes_accessed=100 * 2**20, transcendentals=0),
    )(own)


def merge_stats(pairs):
    devices = pairs.shape[0]
    cells = FRAMES * OWN
    means = pairs[:, 0]
    mean = jnp.sum(means, axis=0, keepdims=True) * (1.0 / devices)
    off = means - mean
    spread = jnp.sum(pairs[:, 1] + off * off * float(cells), axis=0, keepdims=True)
    both = jnp.concatenate([mean, spread], axis=0)
    lane = lax.broadcasted_iota(jnp.int32, (2, C), 1)
    count = float(cells * devices)
    step = 1
    while step < MEMBERS:
        other = jnp.where((lane & step) != 0, pltpu.roll(both, step, 1), pltpu.roll(both, C - step, 1))
        gap = both[0:1] - other[0:1]
        mean = 0.5 * (both[0:1] + other[0:1])
        spread = both[1:2] + other[1:2] + gap * gap * (0.5 * count)
        both = jnp.concatenate([mean, spread], axis=0)
        count *= 2.0
        step *= 2
    return both[0:1], both[1:2] * (1.0 / count)


def border_kernel(own, prev, bottom, top):
    bottom[:2] = prev[:, 3 * COLS :]
    bottom[2:] = own[:, 3 * COLS :]
    top[:2] = prev[:, :COLS]
    top[2:] = own[:, :COLS]


def border_rows(own, prev):
    shape = bf16(WINDOWED, COLS, C)
    return pl.pallas_call(
        border_kernel,
        out_shape=(shape, shape),
        in_specs=[VMEM, VMEM],
        out_specs=(VMEM, VMEM),
        compiler_params=pltpu.CompilerParams(vmem_limit_bytes=8 * 2**20),
        cost_estimate=pl.CostEstimate(flops=10**10, bytes_accessed=200 * 2**20, transcendentals=0),
    )(own, prev)


def activate(values, mean, scale, shift):
    normed = (values.astype(jnp.float32) - mean) * scale + shift
    half = 0.5 * normed
    return half + half * jnp.tanh(half)


def accumulate(sums, taps, slab, frame, finish):
    cells = BLOCK * INNER
    column = lax.rem(lax.broadcasted_iota(jnp.int32, (cells, 1), 0), COLS)
    for s in range(BLOCK + 2):
        frame(s)
    for t in range(0, FRAMES, BLOCK):
        for p in range(3):
            for q in range(3):
                held = taps(3 * p + q, t == 0)
                part = slab(t + p, q).reshape(cells, C)
                for r in range(3):
                    term = jnp.dot(part, held[r], preferred_element_type=jnp.float32)
                    if p == 0 and q == 0:
                        sums[r] = term
                    else:
                        sums[r] += term
        left = jnp.where(column == 0, 0.0, pltpu.roll(sums[0], 1, 0))
        right = jnp.where(column == COLS - 1, 0.0, pltpu.roll(sums[2], cells - 1, 0))
        finish(t, (left + sums[1] + right).reshape(BLOCK, INNER, C))
        for s in range(t + BLOCK + 2, min(t + 2 * BLOCK + 2, WINDOWED)):
            frame(s)


def inner_kernel(place, pairs, gain, bias, own, prev, latents, weight, out, middle, ends, coef, held, tall, sums, sems):
    copies = [
        pltpu.make_async_copy(weight.at[i // 3, i % 3], held.at[i], sems.at[i])
        for i in range(TAPS)
    ]
    for copy in copies[:WINDOW]:
        copy.start()
    mean, variance = merge_stats(pairs[...])
    scale = gain[...] / jnp.sqrt(variance + 1e-06)
    shift = bias[...]
    coef[...] = jnp.concatenate([mean, scale, shift], axis=0)
    first = place[0] == 0

    def taps(i, once):
        if once:
            copies[i].wait()
            if i + WINDOW < TAPS:
                copies[i + WINDOW].start()
        return held.at[i]

    def frame(s):
        values = jnp.where(first, own[0], prev[s]) if s < 2 else own[s - 2]
        values = activate(values, mean, scale, shift)
        tall[s] = values.astype(jnp.bfloat16)
        middle[s] = values[COLS : 3 * COLS].astype(jnp.bfloat16)
        ends[s] = jnp.concatenate([values[:COLS], values[3 * COLS :]], axis=0).astype(jnp.bfloat16)

    def slab(s, q):
        if q == 1:
            return middle[s : s + BLOCK]
        return tall[s : s + BLOCK, q * COLS : q * COLS + INNER]

    def finish(t, total):
        skip = latents[t : t + BLOCK].astype(jnp.float32)[:, COLS : 3 * COLS]
        out[t : t + BLOCK] = (total + skip).astype(jnp.bfloat16)

    accumulate(sums, taps, slab, frame, finish)


def inner_call(place, pairs, gain, bias, own, prev, latents, weight):
    return pl.pallas_call(
        inner_kernel,
        out_shape=(
            bf16(FRAMES, INNER, C),
            bf16(WINDOWED, INNER, C),
            bf16(WINDOWED, INNER, C),
            jax.ShapeDtypeStruct((3, C), jnp.float32),
            bf16(TAPS, 3, C, C),
        ),
        in_specs=[SMALL] + [VMEM] * 6 + [HBM],
        out_specs=(VMEM,) * 5,
        scratch_shapes=[
            pltpu.VMEM((WINDOWED, OWN, C), jnp.bfloat16),
            pltpu.VMEM((3, BLOCK * INNER, C), jnp.float32),
            pltpu.SemaphoreType.DMA((TAPS,)),
        ],
        compiler_params=pltpu.CompilerParams(vmem_limit_bytes=28 * 2**20),
        cost_estimate=pl.CostEstimate(
            flops=FRAMES * INNER * 27 * C * C * 2, bytes_accessed=20 * 2**20, transcendentals=0
        ),
    )(place, pairs, gain, bias, own, prev, latents, weight)


def outer_kernel(place, coef, up, down, latents, inner, middle, ends, held, out, above_two, below_two, sums):
    mean, scale, shift = coef[0:1], coef[1:2], coef[2:3]
    first = place[0] == 0
    keep_up = jnp.where(place[1] == 0, 0.0, 1.0)
    keep_down = jnp.where(place[1] == ROW_SHARDS - 1, 0.0, 1.0)

    def taps(i, once):
        return held.at[i]

    def frame(s):
        above, below = up[s], down[s]
        if s < 2:
            above, below = jnp.where(first, up[2], above), jnp.where(first, down[2], below)
        above = activate(above, mean, scale, shift) * keep_up
        below = activate(below, mean, scale, shift) * keep_down
        between = middle[s].astype(jnp.float32)
        above_two[s] = jnp.concatenate([above, between[COLS:]], axis=0).astype(jnp.bfloat16)
        below_two[s] = jnp.concatenate([between[:COLS], below], axis=0).astype(jnp.bfloat16)

    def slab(s, q):
        return (above_two, ends, below_two)[q][s : s + BLOCK]

    def finish(t, total):
        skip = latents[t : t + BLOCK].astype(jnp.float32)
        top = total[:, :COLS] + skip[:, :COLS]
        bottom = total[:, COLS:] + skip[:, 3 * COLS :]
        between = inner[t : t + BLOCK].astype(jnp.float32)
        out[t : t + BLOCK] = jnp.concatenate([top, between, bottom], axis=1).astype(jnp.bfloat16)

    accumulate(sums, taps, slab, frame, finish)


def outer_call(*operands):
    return pl.pallas_call(
        outer_kernel,
        out_shape=bf16(FRAMES, OWN, C),
        in_specs=[SMALL] + [VMEM] * 8,
        out_specs=VMEM,
        scratch_shapes=[
            pltpu.VMEM((WINDOWED, INNER, C), jnp.bfloat16),
            pltpu.VMEM((WINDOWED, INNER, C), jnp.bfloat16),
            pltpu.VMEM((3, BLOCK * INNER, C), jnp.float32),
        ],
        compiler_params=pltpu.CompilerParams(vmem_limit_bytes=26 * 2**20),
        cost_estimate=pl.CostEstimate(
            flops=FRAMES * INNER * 27 * C * C * 2, bytes_accessed=20 * 2**20, transcendentals=0
        ),
    )(*operands)


def send(block, by_frame, by_row):
    frames, rows = lax.axis_size("frame"), lax.axis_size("row")
    pairs = []
    for f in range(frames):
        for r in range(rows):
            g, s = f + by_frame, r + by_row
            if 0 <= g < frames and 0 <= s < rows:
                pairs.append((f * rows + r, g * rows + s))
    return lax.ppermute(block, ("frame", "row"), pairs)


def shards(latents, hidden, norm_gain, norm_bias, conv_weight):
    own = hidden.reshape(FRAMES, OWN, C)
    skip = latents.reshape(FRAMES, OWN, C)
    members = lax.axis_size("frame") * lax.axis_size("row")
    copies, last_two = local_stats(own, members)
    prev = send(last_two, 1, 0)
    pairs = lax.all_to_all(copies, ("frame", "row"), 0, 0, tiled=True)
    bottom, top = border_rows(own, prev)
    up = send(bottom, 0, 1)
    down = send(top, 0, -1)
    place = jnp.stack([lax.axis_index("frame"), lax.axis_index("row")]).astype(jnp.int32)
    gain, bias = norm_gain.reshape(1, C), norm_bias.reshape(1, C)
    inner, middle, ends, coef, held = inner_call(place, pairs, gain, bias, own, prev, skip, conv_weight)
    result = outer_call(place, coef, up, down, skip, inner, middle, ends, held)
    return result.reshape(FRAMES, ROWS, COLS, C)


def solution(mesh):
    in_specs = (
        P(("clip", "frame"), "row", None, None),
        P(("clip", "frame"), "row", None, None),
        P(),
        P(),
        P(),
    )
    out_specs = P(("clip", "frame"), "row", None, None)
    return jax.shard_map(shards, mesh=mesh, in_specs=in_specs, out_specs=out_specs, check_vma=False)
```

```python
import functools

import jax
import jax.numpy as jnp
from jax import lax
from jax.experimental import pallas as pl
from jax.experimental.pallas import tpu as pltpu
from jax.sharding import PartitionSpec as P

C = 512
MEMBERS = 16
FRAMES = 8
ROWS = 4
COLS = 40
OWN = ROWS * COLS
INNER = 2 * COLS
BLOCK = 4
ROW_SHARDS = 4
WINDOW = 3
CHUNKS = 4
STATS_LIMIT = 63
TAPS = 9
VMEM = pl.BlockSpec(memory_space=pltpu.VMEM)


HBM = pl.BlockSpec(memory_space=pltpu.HBM)
SMALL = pl.BlockSpec(memory_space=pltpu.SMEM)
WINDOWED = FRAMES + 2


def bf16(*shape):
    return jax.ShapeDtypeStruct(shape, jnp.bfloat16)


def stats_kernel(own, out, tail, held, sems):
    size = FRAMES // CHUNKS
    parts = [slice(k * size, (k + 1) * size) for k in range(CHUNKS)]
    copies = [pltpu.make_async_copy(own.at[part], held.at[part], sems.at[k]) for k, part in enumerate(parts)]
    for copy in copies:
        copy.start()
    cells = size * OWN
    means, spreads = [], []
    for part, copy in zip(parts, copies):
        copy.wait()
        mean = jnp.sum(held[part].reshape(cells, C).astype(jnp.float32), axis=0, keepdims=True) * (1.0 / cells)
        centered = held[part].reshape(cells, C).astype(jnp.float32) - mean
        means.append(mean)
        spreads.append(jnp.sum(centered * centered, axis=0, keepdims=True))
    mean = sum(means) * (1.0 / CHUNKS)
    spread = sum(spreads) + sum((each - mean) * (each - mean) for each in means) * float(cells)
    both = jnp.concatenate([mean, spread], axis=0)
    out[...] = jnp.broadcast_to(both[None], out.shape)
    tail[...] = held[FRAMES - 2 :]


def local_stats(own, copies):
    return pl.pallas_call(
        stats_kernel,
        out_shape=(jax.ShapeDtypeStruct((copies, 2, C), jnp.float32), bf16(2, OWN, C)),
        in_specs=[HBM],
        out_specs=(VMEM, VMEM),
        scratch_shapes=[pltpu.VMEM((FRAMES, OWN, C), jnp.bfloat16), pltpu.SemaphoreType.DMA((CHUNKS,))],
        compiler_params=pltpu.CompilerParams(vmem_limit_bytes=STATS_LIMIT * 2**20),
    )(own)


def merge_stats(pairs):
    devices = pairs.shape[0]
    cells = FRAMES * OWN
    means = pairs[:, 0]
    mean = jnp.sum(means, axis=0, keepdims=True) * (1.0 / devices)
    off = means - mean
    spread = jnp.sum(pairs[:, 1] + off * off * float(cells), axis=0, keepdims=True)
    both = jnp.concatenate([mean, spread], axis=0)
    lane = lax.broadcasted_iota(jnp.int32, (2, C), 1)
    count = float(cells * devices)
    step = 1
    while step < MEMBERS:
        other = jnp.where((lane & step) != 0, pltpu.roll(both, step, 1), pltpu.roll(both, C - step, 1))
        gap = both[0:1] - other[0:1]
        mean = 0.5 * (both[0:1] + other[0:1])
        spread = both[1:2] + other[1:2] + gap * gap * (0.5 * count)
        both = jnp.concatenate([mean, spread], axis=0)
        count *= 2.0
        step *= 2
    return both[0:1], both[1:2] * (1.0 / count)


def border_kernel(own, prev, bottom, top):
    bottom[:2] = prev[:, 3 * COLS :]
    bottom[2:] = own[:, 3 * COLS :]
    top[:2] = prev[:, :COLS]
    top[2:] = own[:, :COLS]


def border_rows(own, prev):
    shape = bf16(WINDOWED, COLS, C)
    return pl.pallas_call(
        border_kernel,
        out_shape=(shape, shape),
        in_specs=[VMEM, VMEM],
        out_specs=(VMEM, VMEM),
        compiler_params=pltpu.CompilerParams(vmem_limit_bytes=8 * 2**20),
        cost_estimate=pl.CostEstimate(flops=10**10, bytes_accessed=200 * 2**20, transcendentals=0),
    )(own, prev)


def activate(values, mean, scale, shift):
    normed = (values.astype(jnp.float32) - mean) * scale + shift
    half = 0.5 * normed
    return half + half * jnp.tanh(half)


def accumulate(sums, taps, slab, frame, finish):
    cells = BLOCK * INNER
    column = lax.rem(lax.broadcasted_iota(jnp.int32, (cells, 1), 0), COLS)
    for s in range(BLOCK + 2):
        frame(s)
    for t in range(0, FRAMES, BLOCK):
        held_sums = sums.at[t // BLOCK]
        total = [None] * 3
        for i in range(TAPS):
            held = taps(i, t == 0)
            part = slab(t + i // 3, i % 3).reshape(cells, C)
            for r in range(3):
                term = jnp.dot(part, held[r], preferred_element_type=jnp.float32)
                if i == 0:
                    held_sums[r] = term
                elif i < TAPS - 1:
                    held_sums[r] += term
                else:
                    total[r] = held_sums[r] + term
        left = jnp.where(column == 0, 0.0, pltpu.roll(total[0], 1, 0))
        right = jnp.where(column == COLS - 1, 0.0, pltpu.roll(total[2], cells - 1, 0))
        finish(t, (left + total[1] + right).reshape(BLOCK, INNER, C))
        for s in range(t + BLOCK + 2, min(t + 2 * BLOCK + 2, WINDOWED)):
            frame(s)


def inner_kernel(place, pairs, gain, bias, own, prev, latents, weight, out, middle, ends, coef, held, tall, sums, sems):
    copies = [
        pltpu.make_async_copy(weight.at[i // 3, i % 3], held.at[i], sems.at[i])
        for i in range(TAPS)
    ]
    for copy in copies[:WINDOW]:
        copy.start()
    mean, variance = merge_stats(pairs[...])
    scale = gain[...] / jnp.sqrt(variance + 1e-06)
    shift = bias[...]
    coef[...] = jnp.concatenate([mean, scale, shift], axis=0)
    first = place[0] == 0

    def taps(i, once):
        if once:
            copies[i].wait()
            if i + WINDOW < TAPS:
                copies[i + WINDOW].start()
        return held.at[i]

    def frame(s):
        values = jnp.where(first, own[0], prev[s]) if s < 2 else own[s - 2]
        values = activate(values, mean, scale, shift)
        tall[s] = values.astype(jnp.bfloat16)
        middle[s] = values[COLS : 3 * COLS].astype(jnp.bfloat16)
        ends[s] = jnp.concatenate([values[:COLS], values[3 * COLS :]], axis=0).astype(jnp.bfloat16)

    def slab(s, q):
        if q == 1:
            return middle[s : s + BLOCK]
        return tall[s : s + BLOCK, q * COLS : q * COLS + INNER]

    def finish(t, total):
        skip = latents[t : t + BLOCK].astype(jnp.float32)[:, COLS : 3 * COLS]
        out[t : t + BLOCK] = (total + skip).astype(jnp.bfloat16)

    accumulate(sums, taps, slab, frame, finish)


def inner_call(place, pairs, gain, bias, own, prev, latents, weight):
    return pl.pallas_call(
        inner_kernel,
        out_shape=(
            bf16(FRAMES, INNER, C),
            bf16(WINDOWED, INNER, C),
            bf16(WINDOWED, INNER, C),
            jax.ShapeDtypeStruct((3, C), jnp.float32),
            bf16(TAPS, 3, C, C),
        ),
        in_specs=[SMALL] + [VMEM] * 6 + [HBM],
        out_specs=(VMEM,) * 5,
        scratch_shapes=[
            pltpu.VMEM((WINDOWED, OWN, C), jnp.bfloat16),
            pltpu.VMEM((FRAMES // BLOCK, 3, BLOCK * INNER, C), jnp.float32),
            pltpu.SemaphoreType.DMA((TAPS,)),
        ],
        compiler_params=pltpu.CompilerParams(vmem_limit_bytes=28 * 2**20),
        cost_estimate=pl.CostEstimate(
            flops=FRAMES * INNER * 27 * C * C * 2, bytes_accessed=20 * 2**20, transcendentals=0
        ),
    )(place, pairs, gain, bias, own, prev, latents, weight)


def outer_kernel(place, coef, up, down, latents, inner, middle, ends, held, out, above_two, below_two, sums, done, sems):
    mean, scale, shift = coef[0:1], coef[1:2], coef[2:3]
    first = place[0] == 0
    keep_up = jnp.where(place[1] == 0, 0.0, 1.0)
    keep_down = jnp.where(place[1] == ROW_SHARDS - 1, 0.0, 1.0)

    def taps(i, once):
        return held.at[i]

    def frame(s):
        above, below = up[s], down[s]
        if s < 2:
            above, below = jnp.where(first, up[2], above), jnp.where(first, down[2], below)
        above = activate(above, mean, scale, shift) * keep_up
        below = activate(below, mean, scale, shift) * keep_down
        between = middle[s].astype(jnp.float32)
        above_two[s] = jnp.concatenate([above, between[COLS:]], axis=0).astype(jnp.bfloat16)
        below_two[s] = jnp.concatenate([between[:COLS], below], axis=0).astype(jnp.bfloat16)

    def slab(s, q):
        return (above_two, ends, below_two)[q][s : s + BLOCK]

    def finish(t, total):
        skip = latents[t : t + BLOCK].astype(jnp.float32)
        top = total[:, :COLS] + skip[:, :COLS]
        bottom = total[:, COLS:] + skip[:, 3 * COLS :]
        between = inner[t : t + BLOCK].astype(jnp.float32)
        done[t : t + BLOCK] = jnp.concatenate([top, between, bottom], axis=1).astype(jnp.bfloat16)
        leave(t).start()

    def leave(t):
        return pltpu.make_async_copy(done.at[t : t + BLOCK], out.at[t : t + BLOCK], sems.at[t // BLOCK])

    accumulate(sums, taps, slab, frame, finish)
    for t in range(0, FRAMES, BLOCK):
        leave(t).wait()


def outer_call(*operands):
    return pl.pallas_call(
        outer_kernel,
        out_shape=bf16(FRAMES, OWN, C),
        in_specs=[SMALL] + [VMEM] * 8,
        out_specs=HBM,
        scratch_shapes=[
            pltpu.VMEM((WINDOWED, INNER, C), jnp.bfloat16),
            pltpu.VMEM((WINDOWED, INNER, C), jnp.bfloat16),
            pltpu.VMEM((FRAMES // BLOCK, 3, BLOCK * INNER, C), jnp.float32),
            pltpu.VMEM((FRAMES, OWN, C), jnp.bfloat16),
            pltpu.SemaphoreType.DMA((FRAMES // BLOCK,)),
        ],
        compiler_params=pltpu.CompilerParams(vmem_limit_bytes=26 * 2**20),
        cost_estimate=pl.CostEstimate(
            flops=FRAMES * INNER * 27 * C * C * 2, bytes_accessed=20 * 2**20, transcendentals=0
        ),
    )(*operands)


def send(block, axis, by):
    size = lax.axis_size(axis)
    return lax.ppermute(block, axis, [(i, (i + by) % size) for i in range(size)])


def shards(latents, hidden, norm_gain, norm_bias, conv_weight):
    own = hidden.reshape(FRAMES, OWN, C)
    skip = latents.reshape(FRAMES, OWN, C)
    members = lax.axis_size("frame") * lax.axis_size("row")
    copies, last_two = local_stats(own, members)
    prev = send(last_two, "frame", 1)
    pairs = lax.all_to_all(copies, ("frame", "row"), 0, 0, tiled=True)
    bottom, top = border_rows(own, prev)
    up = send(bottom, "row", 1)
    down = send(top, "row", -1)
    place = jnp.stack([lax.axis_index("frame"), lax.axis_index("row")]).astype(jnp.int32)
    gain, bias = norm_gain.reshape(1, C), norm_bias.reshape(1, C)
    inner, middle, ends, coef, held = inner_call(place, pairs, gain, bias, own, prev, skip, conv_weight)
    result = outer_call(place, coef, up, down, skip, inner, middle, ends, held)
    return result.reshape(FRAMES, ROWS, COLS, C)


def solution(mesh):
    in_specs = (
        P(("clip", "frame"), "row", None, None),
        P(("clip", "frame"), "row", None, None),
        P(),
        P(),
        P(),
    )
    out_specs = P(("clip", "frame"), "row", None, None)
    return jax.shard_map(shards, mesh=mesh, in_specs=in_specs, out_specs=out_specs, check_vma=False)
```

```python
import functools

import jax
import jax.numpy as jnp
from jax import lax
from jax.experimental import pallas as pl
from jax.experimental.pallas import tpu as pltpu
from jax.sharding import PartitionSpec as P

C = 512
MEMBERS = 16
FRAMES = 8
ROWS = 4
COLS = 40
OWN = ROWS * COLS
INNER = 2 * COLS
BLOCK = 4
ROW_SHARDS = 4
WINDOW = 3
CHUNKS = 4
PIECE = 2
STATS_LIMIT = 63
TAPS = 9
VMEM = pl.BlockSpec(memory_space=pltpu.VMEM)


HBM = pl.BlockSpec(memory_space=pltpu.HBM)
SMALL = pl.BlockSpec(memory_space=pltpu.SMEM)
WINDOWED = FRAMES + 2


def bf16(*shape):
    return jax.ShapeDtypeStruct(shape, jnp.bfloat16)


def stats_kernel(own, out, tail, held, sems, leave):
    size = FRAMES // CHUNKS
    parts = [slice(k * size, (k + 1) * size) for k in reversed(range(CHUNKS))]
    copies = [pltpu.make_async_copy(own.at[part], held.at[part], sems.at[k]) for k, part in enumerate(parts)]
    for copy in copies:
        copy.start()
    cells = size * OWN
    means, spreads = [], []
    last_two = pltpu.make_async_copy(held.at[FRAMES - 2 :], tail, leave.at[0])
    for k, (part, copy) in enumerate(zip(parts, copies)):
        copy.wait()
        if k == 0:
            last_two.start()
        mean = jnp.sum(held[part].reshape(cells, C).astype(jnp.float32), axis=0, keepdims=True) * (1.0 / cells)
        centered = held[part].reshape(cells, C).astype(jnp.float32) - mean
        means.append(mean)
        spreads.append(jnp.sum(centered * centered, axis=0, keepdims=True))
    mean = sum(means) * (1.0 / CHUNKS)
    spread = sum(spreads) + sum((each - mean) * (each - mean) for each in means) * float(cells)
    both = jnp.concatenate([mean, spread], axis=0)
    out[...] = jnp.broadcast_to(both[None], out.shape)
    last_two.wait()


def local_stats(own, copies):
    return pl.pallas_call(
        stats_kernel,
        out_shape=(jax.ShapeDtypeStruct((copies, 2, C), jnp.float32), bf16(2, OWN, C)),
        in_specs=[HBM],
        out_specs=(VMEM, HBM),
        scratch_shapes=[pltpu.VMEM((FRAMES, OWN, C), jnp.bfloat16), pltpu.SemaphoreType.DMA((CHUNKS,)), pltpu.SemaphoreType.DMA((1,))],
        compiler_params=pltpu.CompilerParams(vmem_limit_bytes=STATS_LIMIT * 2**20),
    )(own)


def merge_stats(pairs):
    devices = pairs.shape[0]
    cells = FRAMES * OWN
    means = pairs[:, 0]
    mean = jnp.sum(means, axis=0, keepdims=True) * (1.0 / devices)
    off = means - mean
    spread = jnp.sum(pairs[:, 1] + off * off * float(cells), axis=0, keepdims=True)
    both = jnp.concatenate([mean, spread], axis=0)
    lane = lax.broadcasted_iota(jnp.int32, (2, C), 1)
    count = float(cells * devices)
    step = 1
    while step < MEMBERS:
        other = jnp.where((lane & step) != 0, pltpu.roll(both, step, 1), pltpu.roll(both, C - step, 1))
        gap = both[0:1] - other[0:1]
        mean = 0.5 * (both[0:1] + other[0:1])
        spread = both[1:2] + other[1:2] + gap * gap * (0.5 * count)
        both = jnp.concatenate([mean, spread], axis=0)
        count *= 2.0
        step *= 2
    return both[0:1], both[1:2] * (1.0 / count)


def border_kernel(own, prev, bottom, top):
    bottom[:2] = prev[:, 3 * COLS :]
    bottom[2:] = own[:, 3 * COLS :]
    top[:2] = prev[:, :COLS]
    top[2:] = own[:, :COLS]


def border_rows(own, prev):
    shape = bf16(WINDOWED, COLS, C)
    return pl.pallas_call(
        border_kernel,
        out_shape=(shape, shape),
        in_specs=[VMEM, VMEM],
        out_specs=(VMEM, VMEM),
        compiler_params=pltpu.CompilerParams(vmem_limit_bytes=8 * 2**20),
        cost_estimate=pl.CostEstimate(flops=10**10, bytes_accessed=200 * 2**20, transcendentals=0),
    )(own, prev)


def activate(values, mean, scale, shift):
    normed = (values.astype(jnp.float32) - mean) * scale + shift
    half = 0.5 * normed
    return half + half * jnp.tanh(half)


def accumulate(sums, taps, slab, frame, finish):
    cells = BLOCK * INNER
    column = lax.rem(lax.broadcasted_iota(jnp.int32, (cells, 1), 0), COLS)
    for s in range(BLOCK + 2):
        frame(s)
    for t in range(0, FRAMES, BLOCK):
        held_sums = sums.at[t // BLOCK]
        total = [None] * 3
        for i in range(TAPS):
            held = taps(i, t == 0)
            part = slab(t + i // 3, i % 3).reshape(cells, C)
            for r in range(3):
                term = jnp.dot(part, held[r], preferred_element_type=jnp.float32)
                if i == 0:
                    held_sums[r] = term
                elif i < TAPS - 1:
                    held_sums[r] += term
                else:
                    total[r] = held_sums[r] + term
        left = jnp.where(column == 0, 0.0, pltpu.roll(total[0], 1, 0))
        right = jnp.where(column == COLS - 1, 0.0, pltpu.roll(total[2], cells - 1, 0))
        finish(t, (left + total[1] + right).reshape(BLOCK, INNER, C))
        for s in range(t + BLOCK + 2, min(t + 2 * BLOCK + 2, WINDOWED)):
            frame(s)


def inner_kernel(place, pairs, gain, bias, own, prev, latents, weight, out, middle, ends, coef, held, tall, sums, sems):
    copies = [
        pltpu.make_async_copy(weight.at[i // 3, i % 3], held.at[i], sems.at[i])
        for i in range(TAPS)
    ]
    for copy in copies[:WINDOW]:
        copy.start()
    mean, variance = merge_stats(pairs[...])
    scale = gain[...] / jnp.sqrt(variance + 1e-06)
    shift = bias[...]
    coef[...] = jnp.concatenate([mean, scale, shift], axis=0)
    first = place[0] == 0

    def taps(i, once):
        if once:
            copies[i].wait()
            if i + WINDOW < TAPS:
                copies[i + WINDOW].start()
        return held.at[i]

    def frame(s):
        values = jnp.where(first, own[0], prev[s]) if s < 2 else own[s - 2]
        values = activate(values, mean, scale, shift)
        tall[s] = values.astype(jnp.bfloat16)
        middle[s] = values[COLS : 3 * COLS].astype(jnp.bfloat16)
        ends[s] = jnp.concatenate([values[:COLS], values[3 * COLS :]], axis=0).astype(jnp.bfloat16)

    def slab(s, q):
        if q == 1:
            return middle[s : s + BLOCK]
        return tall[s : s + BLOCK, q * COLS : q * COLS + INNER]

    def finish(t, total):
        skip = latents[t : t + BLOCK].astype(jnp.float32)[:, COLS : 3 * COLS]
        out[t : t + BLOCK] = (total + skip).astype(jnp.bfloat16)

    accumulate(sums, taps, slab, frame, finish)


def inner_call(place, pairs, gain, bias, own, prev, latents, weight):
    return pl.pallas_call(
        inner_kernel,
        out_shape=(
            bf16(FRAMES, INNER, C),
            bf16(WINDOWED, INNER, C),
            bf16(WINDOWED, INNER, C),
            jax.ShapeDtypeStruct((3, C), jnp.float32),
            bf16(TAPS, 3, C, C),
        ),
        in_specs=[SMALL] + [VMEM] * 6 + [HBM],
        out_specs=(VMEM,) * 5,
        scratch_shapes=[
            pltpu.VMEM((WINDOWED, OWN, C), jnp.bfloat16),
            pltpu.VMEM((FRAMES // BLOCK, 3, BLOCK * INNER, C), jnp.float32),
            pltpu.SemaphoreType.DMA((TAPS,)),
        ],
        compiler_params=pltpu.CompilerParams(vmem_limit_bytes=28 * 2**20),
        cost_estimate=pl.CostEstimate(
            flops=FRAMES * INNER * 27 * C * C * 2, bytes_accessed=20 * 2**20, transcendentals=0
        ),
    )(place, pairs, gain, bias, own, prev, latents, weight)


def outer_kernel(place, coef, up, down, latents, inner, middle, ends, held, out, above_two, below_two, sums, done, sems):
    mean, scale, shift = coef[0:1], coef[1:2], coef[2:3]
    first = place[0] == 0
    keep_up = jnp.where(place[1] == 0, 0.0, 1.0)
    keep_down = jnp.where(place[1] == ROW_SHARDS - 1, 0.0, 1.0)

    def taps(i, once):
        return held.at[i]

    def frame(s):
        above, below = up[s], down[s]
        if s < 2:
            above, below = jnp.where(first, up[2], above), jnp.where(first, down[2], below)
        above = activate(above, mean, scale, shift) * keep_up
        below = activate(below, mean, scale, shift) * keep_down
        between = middle[s].astype(jnp.float32)
        above_two[s] = jnp.concatenate([above, between[COLS:]], axis=0).astype(jnp.bfloat16)
        below_two[s] = jnp.concatenate([between[:COLS], below], axis=0).astype(jnp.bfloat16)

    def slab(s, q):
        return (above_two, ends, below_two)[q][s : s + BLOCK]

    def finish(t, total):
        for u in range(t, t + BLOCK, PIECE):
            piece = total[u - t : u - t + PIECE]
            skip = latents[u : u + PIECE].astype(jnp.float32)
            top = piece[:, :COLS] + skip[:, :COLS]
            bottom = piece[:, COLS:] + skip[:, 3 * COLS :]
            between = inner[u : u + PIECE].astype(jnp.float32)
            done[u : u + PIECE] = jnp.concatenate([top, between, bottom], axis=1).astype(jnp.bfloat16)
            leave(u).start()

    def leave(u):
        return pltpu.make_async_copy(done.at[u : u + PIECE], out.at[u : u + PIECE], sems.at[u // PIECE])

    accumulate(sums, taps, slab, frame, finish)
    for u in range(0, FRAMES, PIECE):
        leave(u).wait()


def outer_call(*operands):
    return pl.pallas_call(
        outer_kernel,
        out_shape=bf16(FRAMES, OWN, C),
        in_specs=[SMALL] + [VMEM] * 8,
        out_specs=HBM,
        scratch_shapes=[
            pltpu.VMEM((WINDOWED, INNER, C), jnp.bfloat16),
            pltpu.VMEM((WINDOWED, INNER, C), jnp.bfloat16),
            pltpu.VMEM((FRAMES // BLOCK, 3, BLOCK * INNER, C), jnp.float32),
            pltpu.VMEM((FRAMES, OWN, C), jnp.bfloat16),
            pltpu.SemaphoreType.DMA((FRAMES // PIECE,)),
        ],
        compiler_params=pltpu.CompilerParams(vmem_limit_bytes=26 * 2**20),
        cost_estimate=pl.CostEstimate(
            flops=FRAMES * INNER * 27 * C * C * 2, bytes_accessed=20 * 2**20, transcendentals=0
        ),
    )(*operands)


def send(block, axis, by):
    size = lax.axis_size(axis)
    return lax.ppermute(block, axis, [(i, (i + by) % size) for i in range(size)])


def shards(latents, hidden, norm_gain, norm_bias, conv_weight):
    own = hidden.reshape(FRAMES, OWN, C)
    skip = latents.reshape(FRAMES, OWN, C)
    members = lax.axis_size("frame") * lax.axis_size("row")
    copies, last_two = local_stats(own, members)
    prev = send(last_two, "frame", 1)
    pairs = lax.all_to_all(copies, ("frame", "row"), 0, 0, tiled=True)
    bottom, top = border_rows(own, prev)
    up = send(bottom, "row", 1)
    down = send(top, "row", -1)
    place = jnp.stack([lax.axis_index("frame"), lax.axis_index("row")]).astype(jnp.int32)
    gain, bias = norm_gain.reshape(1, C), norm_bias.reshape(1, C)
    inner, middle, ends, coef, held = inner_call(place, pairs, gain, bias, own, prev, skip, conv_weight)
    result = outer_call(place, coef, up, down, skip, inner, middle, ends, held)
    return result.reshape(FRAMES, ROWS, COLS, C)


def solution(mesh):
    in_specs = (
        P(("clip", "frame"), "row", None, None),
        P(("clip", "frame"), "row", None, None),
        P(),
        P(),
        P(),
    )
    out_specs = P(("clip", "frame"), "row", None, None)
    return jax.shard_map(shards, mesh=mesh, in_specs=in_specs, out_specs=out_specs, check_vma=False)
```

```python
import functools

import jax
import jax.numpy as jnp
from jax import lax
from jax.experimental import pallas as pl
from jax.experimental.pallas import tpu as pltpu
from jax.sharding import PartitionSpec as P

C = 512
MEMBERS = 16
FRAMES = 8
ROWS = 4
COLS = 40
OWN = ROWS * COLS
INNER = 2 * COLS
BLOCK = 4
ROW_SHARDS = 4
WINDOW = 3
CHUNKS = 4
PIECE = 2
STATS_LIMIT = 63
TAPS = 9
VMEM = pl.BlockSpec(memory_space=pltpu.VMEM)


HBM = pl.BlockSpec(memory_space=pltpu.HBM)
SMALL = pl.BlockSpec(memory_space=pltpu.SMEM)
WINDOWED = FRAMES + 2


def bf16(*shape):
    return jax.ShapeDtypeStruct(shape, jnp.bfloat16)


def stats_kernel(own, out, tail, held, sems, leave):
    size = FRAMES // CHUNKS
    parts = [slice(k * size, (k + 1) * size) for k in reversed(range(CHUNKS))]
    copies = [pltpu.make_async_copy(own.at[part], held.at[part], sems.at[k]) for k, part in enumerate(parts)]
    for copy in copies:
        copy.start()
    cells = size * OWN
    means, spreads = [], []
    last_two = pltpu.make_async_copy(held.at[FRAMES - 2 :], tail, leave.at[0])
    for k, (part, copy) in enumerate(zip(parts, copies)):
        copy.wait()
        if k == 0:
            last_two.start()
        mean = jnp.sum(held[part].reshape(cells, C).astype(jnp.float32), axis=0, keepdims=True) * (1.0 / cells)
        centered = held[part].reshape(cells, C).astype(jnp.float32) - mean
        means.append(mean)
        spreads.append(jnp.sum(centered * centered, axis=0, keepdims=True))
    mean = sum(means) * (1.0 / CHUNKS)
    spread = sum(spreads) + sum((each - mean) * (each - mean) for each in means) * float(cells)
    both = jnp.concatenate([mean, spread], axis=0)
    out[...] = jnp.broadcast_to(both[None], out.shape)
    last_two.wait()


def local_stats(own, copies):
    return pl.pallas_call(
        stats_kernel,
        out_shape=(jax.ShapeDtypeStruct((copies, 2, C), jnp.float32), bf16(2, OWN, C)),
        in_specs=[HBM],
        out_specs=(VMEM, HBM),
        scratch_shapes=[pltpu.VMEM((FRAMES, OWN, C), jnp.bfloat16), pltpu.SemaphoreType.DMA((CHUNKS,)), pltpu.SemaphoreType.DMA((1,))],
        compiler_params=pltpu.CompilerParams(vmem_limit_bytes=STATS_LIMIT * 2**20),
    )(own)


def merge_stats(pairs):
    devices = pairs.shape[0]
    cells = FRAMES * OWN
    means = pairs[:, 0]
    mean = jnp.sum(means, axis=0, keepdims=True) * (1.0 / devices)
    off = means - mean
    spread = jnp.sum(pairs[:, 1] + off * off * float(cells), axis=0, keepdims=True)
    both = jnp.concatenate([mean, spread], axis=0)
    lane = lax.broadcasted_iota(jnp.int32, (2, C), 1)
    count = float(cells * devices)
    step = 1
    while step < MEMBERS:
        other = jnp.where((lane & step) != 0, pltpu.roll(both, step, 1), pltpu.roll(both, C - step, 1))
        gap = both[0:1] - other[0:1]
        mean = 0.5 * (both[0:1] + other[0:1])
        spread = both[1:2] + other[1:2] + gap * gap * (0.5 * count)
        both = jnp.concatenate([mean, spread], axis=0)
        count *= 2.0
        step *= 2
    return both[0:1], both[1:2] * (1.0 / count)


def border_kernel(own, prev, bottom, top):
    bottom[:2] = prev[:, 3 * COLS :]
    bottom[2:] = own[:, 3 * COLS :]
    top[:2] = prev[:, :COLS]
    top[2:] = own[:, :COLS]


def border_rows(own, prev):
    shape = bf16(WINDOWED, COLS, C)
    return pl.pallas_call(
        border_kernel,
        out_shape=(shape, shape),
        in_specs=[VMEM, VMEM],
        out_specs=(VMEM, VMEM),
        compiler_params=pltpu.CompilerParams(vmem_limit_bytes=8 * 2**20),
        cost_estimate=pl.CostEstimate(flops=10**10, bytes_accessed=200 * 2**20, transcendentals=0),
    )(own, prev)


def activate(values, mean, scale, shift):
    normed = (values.astype(jnp.float32) - mean) * scale + shift
    half = 0.5 * normed
    return half + half * jnp.tanh(half)


def accumulate(sums, taps, slab, frame, finish):
    cells = BLOCK * INNER
    column = lax.rem(lax.broadcasted_iota(jnp.int32, (cells, 1), 0), COLS)
    for s in range(BLOCK + 2):
        frame(s)
    for t in range(0, FRAMES, BLOCK):
        held_sums = sums.at[t // BLOCK]
        total = [None] * 3
        for i in range(TAPS):
            part = slab(t + i // 3, i % 3).reshape(cells, C)
            for r in range(3):
                term = jnp.dot(part, taps(i, r, t == 0), preferred_element_type=jnp.float32)
                if i == 0:
                    held_sums[r] = term
                elif i < TAPS - 1:
                    held_sums[r] += term
                else:
                    total[r] = held_sums[r] + term
        left = jnp.where(column == 0, 0.0, pltpu.roll(total[0], 1, 0))
        right = jnp.where(column == COLS - 1, 0.0, pltpu.roll(total[2], cells - 1, 0))
        finish(t, (left + total[1] + right).reshape(BLOCK, INNER, C))
        for s in range(t + BLOCK + 2, min(t + 2 * BLOCK + 2, WINDOWED)):
            frame(s)


def inner_kernel(place, pairs, gain, bias, own, prev, latents, weight, out, middle, ends, coef, held, tall, sums, sems):
    copies = [
        pltpu.make_async_copy(weight.at[i // 9, i // 3 % 3, i % 3], held.at[i // 3, i % 3], sems.at[i])
        for i in range(3 * TAPS)
    ]
    for copy in copies[: 3 * WINDOW]:
        copy.start()
    mean, variance = merge_stats(pairs[...])
    scale = gain[...] / jnp.sqrt(variance + 1e-06)
    shift = bias[...]
    coef[...] = jnp.concatenate([mean, scale, shift], axis=0)
    first = place[0] == 0

    def taps(i, r, once):
        if once:
            j = 3 * i + r
            copies[j].wait()
            if j + 3 * WINDOW < 3 * TAPS:
                copies[j + 3 * WINDOW].start()
        return held[i, r]

    def frame(s):
        values = jnp.where(first, own[0], prev[s]) if s < 2 else own[s - 2]
        values = activate(values, mean, scale, shift)
        tall[s] = values.astype(jnp.bfloat16)
        middle[s] = values[COLS : 3 * COLS].astype(jnp.bfloat16)
        ends[s] = jnp.concatenate([values[:COLS], values[3 * COLS :]], axis=0).astype(jnp.bfloat16)

    def slab(s, q):
        if q == 1:
            return middle[s : s + BLOCK]
        return tall[s : s + BLOCK, q * COLS : q * COLS + INNER]

    def finish(t, total):
        skip = latents[t : t + BLOCK].astype(jnp.float32)[:, COLS : 3 * COLS]
        out[t : t + BLOCK] = (total + skip).astype(jnp.bfloat16)

    accumulate(sums, taps, slab, frame, finish)


def inner_call(place, pairs, gain, bias, own, prev, latents, weight):
    return pl.pallas_call(
        inner_kernel,
        out_shape=(
            bf16(FRAMES, INNER, C),
            bf16(WINDOWED, INNER, C),
            bf16(WINDOWED, INNER, C),
            jax.ShapeDtypeStruct((3, C), jnp.float32),
            bf16(TAPS, 3, C, C),
        ),
        in_specs=[SMALL] + [VMEM] * 6 + [HBM],
        out_specs=(VMEM,) * 5,
        scratch_shapes=[
            pltpu.VMEM((WINDOWED, OWN, C), jnp.bfloat16),
            pltpu.VMEM((FRAMES // BLOCK, 3, BLOCK * INNER, C), jnp.float32),
            pltpu.SemaphoreType.DMA((3 * TAPS,)),
        ],
        compiler_params=pltpu.CompilerParams(vmem_limit_bytes=28 * 2**20),
        cost_estimate=pl.CostEstimate(
            flops=FRAMES * INNER * 27 * C * C * 2, bytes_accessed=20 * 2**20, transcendentals=0
        ),
    )(place, pairs, gain, bias, own, prev, latents, weight)


def outer_kernel(place, coef, up, down, latents, inner, middle, ends, held, out, above_two, below_two, sums, done, sems):
    mean, scale, shift = coef[0:1], coef[1:2], coef[2:3]
    first = place[0] == 0
    keep_up = jnp.where(place[1] == 0, 0.0, 1.0)
    keep_down = jnp.where(place[1] == ROW_SHARDS - 1, 0.0, 1.0)

    def taps(i, r, once):
        return held[i, r]

    def frame(s):
        above, below = up[s], down[s]
        if s < 2:
            above, below = jnp.where(first, up[2], above), jnp.where(first, down[2], below)
        above = activate(above, mean, scale, shift) * keep_up
        below = activate(below, mean, scale, shift) * keep_down
        between = middle[s].astype(jnp.float32)
        above_two[s] = jnp.concatenate([above, between[COLS:]], axis=0).astype(jnp.bfloat16)
        below_two[s] = jnp.concatenate([between[:COLS], below], axis=0).astype(jnp.bfloat16)

    def slab(s, q):
        return (above_two, ends, below_two)[q][s : s + BLOCK]

    def finish(t, total):
        for u in range(t, t + BLOCK, PIECE):
            piece = total[u - t : u - t + PIECE]
            skip = latents[u : u + PIECE].astype(jnp.float32)
            top = piece[:, :COLS] + skip[:, :COLS]
            bottom = piece[:, COLS:] + skip[:, 3 * COLS :]
            between = inner[u : u + PIECE].astype(jnp.float32)
            done[u : u + PIECE] = jnp.concatenate([top, between, bottom], axis=1).astype(jnp.bfloat16)
            leave(u).start()

    def leave(u):
        return pltpu.make_async_copy(done.at[u : u + PIECE], out.at[u : u + PIECE], sems.at[u // PIECE])

    accumulate(sums, taps, slab, frame, finish)
    for u in range(0, FRAMES, PIECE):
        leave(u).wait()


def outer_call(*operands):
    return pl.pallas_call(
        outer_kernel,
        out_shape=bf16(FRAMES, OWN, C),
        in_specs=[SMALL] + [VMEM] * 8,
        out_specs=HBM,
        scratch_shapes=[
            pltpu.VMEM((WINDOWED, INNER, C), jnp.bfloat16),
            pltpu.VMEM((WINDOWED, INNER, C), jnp.bfloat16),
            pltpu.VMEM((FRAMES // BLOCK, 3, BLOCK * INNER, C), jnp.float32),
            pltpu.VMEM((FRAMES, OWN, C), jnp.bfloat16),
            pltpu.SemaphoreType.DMA((FRAMES // PIECE,)),
        ],
        compiler_params=pltpu.CompilerParams(vmem_limit_bytes=26 * 2**20),
        cost_estimate=pl.CostEstimate(
            flops=FRAMES * INNER * 27 * C * C * 2, bytes_accessed=20 * 2**20, transcendentals=0
        ),
    )(*operands)


def send(block, axis, by):
    size = lax.axis_size(axis)
    return lax.ppermute(block, axis, [(i, (i + by) % size) for i in range(size)])


def shards(latents, hidden, norm_gain, norm_bias, conv_weight):
    own = hidden.reshape(FRAMES, OWN, C)
    skip = latents.reshape(FRAMES, OWN, C)
    members = lax.axis_size("frame") * lax.axis_size("row")
    copies, last_two = local_stats(own, members)
    prev = send(last_two, "frame", 1)
    pairs = lax.all_to_all(copies, ("frame", "row"), 0, 0, tiled=True)
    bottom, top = border_rows(own, prev)
    up = send(bottom, "row", 1)
    down = send(top, "row", -1)
    place = jnp.stack([lax.axis_index("frame"), lax.axis_index("row")]).astype(jnp.int32)
    gain, bias = norm_gain.reshape(1, C), norm_bias.reshape(1, C)
    inner, middle, ends, coef, held = inner_call(place, pairs, gain, bias, own, prev, skip, conv_weight)
    result = outer_call(place, coef, up, down, skip, inner, middle, ends, held)
    return result.reshape(FRAMES, ROWS, COLS, C)


def solution(mesh):
    in_specs = (
        P(("clip", "frame"), "row", None, None),
        P(("clip", "frame"), "row", None, None),
        P(),
        P(),
        P(),
    )
    out_specs = P(("clip", "frame"), "row", None, None)
    return jax.shard_map(shards, mesh=mesh, in_specs=in_specs, out_specs=out_specs, check_vma=False)
```
